256 devices in a mesh: row: 32 (over z_hi, y, core), col: 8 (over x, z_lo).
Axes of the slice: x: 4, y: 4, z: 8 (z_hi: 4, z_lo: 2; z = z_hi * 2 + z_lo), core: 2. Of those that a mesh axis runs over, the one named last changes fastest.
Arguments:
- residues: int32 [1024], P('row'), may hold values from 0 to 20
- embed_table: bfloat16 [21, 256], replicated, may hold values from -6 to 6
- conv_first: bfloat16 [4352, 256], replicated, may hold values from -0.09375 to 0.09375
- conv_second: bfloat16 [4352, 256], replicated, may hold values from -0.09375 to 0.09375
- proj_row: bfloat16 [256, 64], replicated, may hold values from -0.375 to 0.375
- proj_col: bfloat16 [256, 64], replicated, may hold values from -0.375 to 0.375
- pair_weights: bfloat16 [4, 64, 576], replicated, may hold values from -0.25 to 0.25
Outputs:
- pair_out: bfloat16 [64, 1024, 1024], P(None, 'row', 'col')
The draws below stay inside these ranges and needn't reach their ends.
All inputs are finite; a program needn't handle non-finite values.
Results may differ from the reference program's by a relative error of at most 0.018.
Values may be sent and summed in bfloat16 or wider, within the bound.
No kernel may reach another device: no remote copies, remote signals or barrier semaphores. Data moves between devices by JAX's collectives and lax.ppermute only.
A program may use at most 64 MiB of HBM per device.

```python
import jax
import jax.numpy as jnp
from jax import lax

W = 256
C = 64
VOCAB = 21
KERNEL = 17
LAYERS = 4
WINDOW = 1024


def place_ends(entries, key, smallest, high):
    index_at = [jax.random.randint(jax.random.fold_in(key, axis), (), 0, length) for axis, length in enumerate(entries.shape)]
    main_axis = entries.shape.index(max(entries.shape))
    neighbour = index_at[:main_axis] + [(index_at[main_axis] + 1) % entries.shape[main_axis]] + index_at[main_axis + 1:]
    return entries.at[tuple(index_at)].set(smallest).at[tuple(neighbour)].set(high)


def scatter_about(stream_key, dims, scale, reach, kind=jnp.bfloat16):
    entries = jax.random.normal(stream_key, dims, jnp.float32) * scale
    return jnp.minimum(jnp.maximum(entries, -reach), reach).astype(kind)


def setup_inputs(seed: int = 0) -> dict:
    key_of = jax.random.split(jax.random.key(seed), 8)
    return {
        "residues": place_ends(jax.random.randint(key_of[0], (WINDOW,), 0, VOCAB), jax.random.fold_in(key_of[0], 1), 0, VOCAB - 1).astype(jnp.int32),
        "embed_table": scatter_about(key_of[1], (VOCAB, W), 1.0, 6.0),
        "conv_first": scatter_about(key_of[2], (KERNEL * W, W), (KERNEL * W) ** -0.5, 0.09375),
        "conv_second": scatter_about(key_of[3], (KERNEL * W, W), (KERNEL * W) ** -0.5, 0.09375),
        "proj_row": scatter_about(key_of[4], (W, C), W ** -0.5, 0.375),
        "proj_col": scatter_about(key_of[5], (W, C), W ** -0.5, 0.375),
        "pair_weights": scatter_about(key_of[6], (LAYERS, C, 9 * C), (9 * C) ** -0.5, 0.25),
    }


def elu(v):
    return jnp.where(v > 0, v, jnp.expm1(jnp.minimum(v, 0.0)))


def conv_seq(feats, weight_stack):
    half = KERNEL // 2
    length = feats.shape[0]
    padded = jnp.pad(feats, ((half, half), (0, 0)))
    windows = jnp.concatenate([padded[k:k + length] for k in range(KERNEL)], axis=1)
    return jnp.dot(windows, weight_stack, preferred_element_type=jnp.float32)


def reference(residues, embed_table, conv_first, conv_second, proj_row, proj_col, pair_weights):
    onehot = (residues[:, None] == jnp.arange(VOCAB, dtype=jnp.int32)[None, :]).astype(jnp.bfloat16)
    embedded = jnp.dot(onehot, embed_table, preferred_element_type=jnp.float32).astype(jnp.bfloat16)
    first = elu(conv_seq(embedded, conv_first)).astype(jnp.bfloat16)
    second = (first.astype(jnp.float32) + elu(conv_seq(first, conv_second))).astype(jnp.bfloat16)
    left = jnp.dot(second, proj_row, preferred_element_type=jnp.float32).astype(jnp.bfloat16)
    right = jnp.dot(second, proj_col, preferred_element_type=jnp.float32).astype(jnp.bfloat16)
    pair_features = (left.T.astype(jnp.float32)[:, :, None] + right.T.astype(jnp.float32)[:, None, :]).astype(jnp.bfloat16)
    for layer_number in range(LAYERS):
        dilation_rate = 2 ** layer_number
        activation_map = elu(pair_features.astype(jnp.float32)).astype(jnp.bfloat16).astype(jnp.float32)
        filter_kernel = pair_weights[layer_number].astype(jnp.float32).reshape(C, 3, 3, C).transpose(0, 3, 1, 2)
        output_map = lax.conv_general_dilated(activation_map[None], filter_kernel, (1, 1), ((dilation_rate, dilation_rate), (dilation_rate, dilation_rate)), rhs_dilation=(dilation_rate, dilation_rate), dimension_numbers=("NCHW", "OIHW", "NCHW"), precision=lax.Precision.HIGHEST)[0]
        pair_features = (pair_features.astype(jnp.float32) + output_map).astype(jnp.bfloat16)
    return pair_features
```

```python
import jax
import jax.numpy as jnp
from jax import lax
from jax.experimental import pallas as pl
from jax.experimental.pallas import tpu as pltpu
from jax.sharding import PartitionSpec as P

KERNEL = 17
HALF = KERNEL // 2
LAYERS = 4
WINDOW = 1024
VOCAB_PAD = 32
ROWS = 32
COLS = 128
HALO = 16
PLANES = ROWS + 2 * HALO
CH = 64
W = 256
f32, bf16 = jnp.float32, jnp.bfloat16


def elu(v):
    return jnp.maximum(v, jnp.exp(jnp.minimum(v, 0.0)) - 1.0)


def tables_kernel(table_ref, w_ref, out_ref):
    parts = [
        jnp.dot(table_ref[...], w_ref[pl.ds(k * W, W), :], preferred_element_type=f32)
        for k in range(KERNEL)
    ]
    out_ref[...] = jnp.concatenate(parts, axis=0).T.astype(bf16)


def pair_kernel(res_ref, tt_ref, w2_ref, pr_ref, pc_ref, pw_ref, out_ref, f_ref, x_ref, a_ref, b_ref, s_ref):
    row0 = lax.axis_index("row") * ROWS
    col0 = lax.axis_index("col") * COLS
    res = res_ref[...]
    span = res.shape[1]

    kinds = lax.broadcasted_iota(jnp.int32, (VOCAB_PAD, span), 0)
    hot = jnp.concatenate(
        [
            jnp.where(pltpu.roll(res, (span - k) % span, 1) == kinds, 1.0, 0.0).astype(bf16)
            for k in range(KERNEL)
        ],
        axis=0,
    )
    first_t = jnp.dot(tt_ref[...], hot, preferred_element_type=f32)
    lane = lax.broadcasted_iota(jnp.int32, (1, span), 1)
    pos = jnp.where(lane < 128, row0 - HALO - HALF + lane, col0 - HALO - HALF + lane - 128)
    first_t = jnp.where((pos >= 0) & (pos < WINDOW), elu(first_t), 0.0)
    f_ref[...] = first_t.T.astype(bf16).astype(f32)

    wide = COLS + 2 * HALO
    acc = jnp.zeros((PLANES + wide, W), f32)
    for k in range(KERNEL):
        lhs = jnp.concatenate([f_ref[pl.ds(k, PLANES), :], f_ref[pl.ds(128 + k, wide), :]], axis=0)
        acc = acc + jnp.dot(lhs.astype(bf16), w2_ref[pl.ds(k * W, W), :], preferred_element_type=f32)
    centre = jnp.concatenate([f_ref[pl.ds(HALF, PLANES), :], f_ref[pl.ds(128 + HALF, wide), :]], axis=0)
    second = (centre + elu(acc)).astype(bf16)

    nt = (((1,), (1,)), ((), ()))
    left = lax.dot_general(pr_ref[...], second[:PLANES], nt, preferred_element_type=f32)
    left = left.astype(bf16).astype(f32)
    starts = (PLANES, PLANES + 2 * HALO)
    right = jnp.concatenate(
        [
            lax.dot_general(pc_ref[...], second[s : s + COLS], nt, preferred_element_type=f32)
            for s in starts
        ],
        axis=1,
    )
    right = right.astype(bf16).astype(f32)

    lane2 = lax.broadcasted_iota(jnp.int32, (1, 2 * COLS), 1)
    col = col0 - HALO + lane2 - jnp.where(lane2 < COLS, 0, COLS - 2 * HALO)
    col_ok = jnp.where((col >= 0) & (col < WINDOW), 1.0, 0.0)

    def mask(plane):
        row = row0 - HALO + plane
        return jnp.where((row >= 0) & (row < WINDOW), col_ok, 0.0)

    def rows_of(plane):
        if isinstance(plane, int):
            return pl.ds(plane * CH, CH)
        return pl.ds(pl.multiple_of(plane * CH, CH), CH)

    for plane in range(1, PLANES - 1):
        x = (left[:, plane : plane + 1] + right).astype(bf16).astype(f32)
        x_ref[rows_of(plane), :] = x
        a_ref[rows_of(plane), :] = (elu(x) * mask(plane)).astype(bf16)

    def layer(number, low, high, src, dst, unroll):
        d = 2**number
        weights = pw_ref[number]

        def one(plane):
            stack = jnp.concatenate([src[rows_of(plane + (t - 1) * d), :] for t in range(3)], axis=0)
            y = jnp.dot(weights, stack, preferred_element_type=f32)
            tiles = []
            for t in range(2):
                part = y[:, t * COLS : (t + 1) * COLS]
                tiles.append(
                    pltpu.roll(part[:CH], d, 1) + part[CH : 2 * CH] + pltpu.roll(part[2 * CH :], COLS - d, 1)
                )
            if dst is None:
                a = tiles[0] + x_ref[rows_of(plane), :COLS]
                b = tiles[1] + x_ref[rows_of(plane), COLS:]
                a = pltpu.roll(a, COLS - HALO, 1)
                b = pltpu.roll(b, HALO, 1)
                lanes = lax.broadcasted_iota(jnp.int32, (1, COLS), 1)
                s_ref[pl.ds(plane - HALO, CH, stride=ROWS), :] = jnp.where(lanes < COLS // 2, a, b)
            else:
                x = x_ref[rows_of(plane), :] + jnp.concatenate(tiles, axis=1)
                x_ref[rows_of(plane), :] = x
                dst[rows_of(plane), :] = (elu(x) * mask(plane)).astype(bf16)

        def body(step, carry):
            for u in range(unroll):
                one(low + step * unroll + u)
            return carry

        lax.fori_loop(0, (high - low) // unroll, body, 0)

    layer(0, 2, 62, a_ref, b_ref, 4)
    layer(1, 4, 60, b_ref, a_ref, 4)
    layer(2, 8, 56, a_ref, b_ref, 4)
    layer(3, 16, 48, b_ref, None, 4)
    out_ref[...] = s_ref[...].reshape(CH, ROWS, COLS).astype(bf16)


def local(residues, embed_table, conv_first, conv_second, proj_row, proj_col, pair_weights):
    row, col = lax.axis_index("row"), lax.axis_index("col")
    copies = jnp.broadcast_to(residues, (lax.axis_size("row"), ROWS))
    every = lax.all_to_all(copies, "row", 0, 0, tiled=True).reshape(-1)
    every = jnp.pad(every, (ROWS, ROWS), constant_values=-1)
    rows_window = lax.dynamic_slice_in_dim(every, row * ROWS, 3 * ROWS)
    cols_window = lax.dynamic_slice_in_dim(every, col * COLS, COLS + 2 * ROWS)
    res = jnp.concatenate([rows_window, jnp.full((32,), -1, jnp.int32), cols_window, jnp.full((64,), -1, jnp.int32)])[None]

    table = jnp.pad(embed_table, ((0, VOCAB_PAD - embed_table.shape[0]), (0, 0)))
    tt = pl.pallas_call(
        tables_kernel,
        out_shape=jax.ShapeDtypeStruct((W, KERNEL * VOCAB_PAD), bf16),
        compiler_params=pltpu.CompilerParams(vmem_limit_bytes=16 * 2**20),
        cost_estimate=pl.CostEstimate(flops=2 * 32 * 4352 * 256, bytes_accessed=3 * 2**20, transcendentals=0),
    )(table, conv_first)
    pw = pair_weights.reshape(LAYERS, CH, 3, 3, CH).transpose(0, 3, 1, 2, 4).reshape(LAYERS, 3 * CH, 3 * CH)
    return pl.pallas_call(
        pair_kernel,
        out_shape=jax.ShapeDtypeStruct((CH, ROWS, COLS), bf16),
        scratch_shapes=[
            pltpu.VMEM((384, W), f32),
            pltpu.VMEM((PLANES * CH, 2 * COLS), f32),
            pltpu.VMEM((PLANES * CH, 2 * COLS), bf16),
            pltpu.VMEM((PLANES * CH, 2 * COLS), bf16),
            pltpu.VMEM((CH * ROWS, COLS), f32),
        ],
        compiler_params=pltpu.CompilerParams(vmem_limit_bytes=40 * 2**20),
        cost_estimate=pl.CostEstimate(flops=2 * 64 * 4096 * 2304, bytes_accessed=4 * 2**20, transcendentals=0),
    )(res, tt, conv_second, proj_row.T, proj_col.T, pw)


def solution(mesh):
    return jax.shard_map(
        local,
        mesh=mesh,
        in_specs=(P("row"), P(), P(), P(), P(), P(), P()),
        out_specs=P(None, "row", "col"),
        check_vma=False,
    )
```

```python
import jax
import jax.numpy as jnp
from jax import lax
from jax.experimental import pallas as pl
from jax.experimental.pallas import tpu as pltpu
from jax.sharding import PartitionSpec as P

KERNEL = 17
HALF = KERNEL // 2
LAYERS = 4
WINDOW = 1024
VOCAB_PAD = 32
PIECES = (0, 5, 9, 13, 17)
ROWS = 32
COLS = 128
HALO = 16
PLANES = ROWS + 2 * HALO
CH = 64
W = 256
f32, bf16 = jnp.float32, jnp.bfloat16


def elu(v):
    return jnp.maximum(v, jnp.exp(jnp.minimum(v, 0.0)) - 1.0)


def tables_kernel(table_ref, w_hbm, out_ref, w_ref, sems):
    copies = [
        pltpu.make_async_copy(w_hbm.at[pl.ds(a * W, (b - a) * W)], w_ref.at[pl.ds(a * W, (b - a) * W)], sems.at[n])
        for n, (a, b) in enumerate(zip(PIECES, PIECES[1:]))
    ]
    for copy in copies:
        copy.start()
    parts = []
    for k in range(KERNEL):
        if k in PIECES:
            copies[PIECES.index(k)].wait()
        parts.append(jnp.dot(table_ref[...], w_ref[pl.ds(k * W, W), :], preferred_element_type=f32))
    out_ref[...] = jnp.concatenate(parts, axis=0).T.astype(bf16)


def pair_kernel(res_ref, tt_ref, w2_ref, pr_ref, pc_ref, pw_ref, out_ref, f_ref, x_ref, a_ref, b_ref, s_ref):
    row, column = lax.axis_index("row"), lax.axis_index("col")
    row0, col0 = row * ROWS, column * COLS
    blocks = res_ref.shape[0]
    span = 384

    def block(number):
        return res_ref[jnp.clip(number, 0, blocks - 1)]

    rows_blocks = [block(row - 1 + t) for t in range(3)]
    cols_blocks = [block(column * (COLS // ROWS) - 1 + t) for t in range(6)]
    res = jnp.concatenate(rows_blocks + rows_blocks[:1] + cols_blocks + cols_blocks[:2], axis=1)
    lane = lax.broadcasted_iota(jnp.int32, (1, span), 1)
    pos = jnp.where(lane < 128, row0 + lane, col0 + lane - 128)
    res = jnp.where((pos >= ROWS) & (pos < WINDOW + ROWS), res, -1)

    kinds = lax.broadcasted_iota(jnp.int32, (VOCAB_PAD, span), 0)
    hot = jnp.concatenate(
        [
            jnp.where(pltpu.roll(res, (span - k) % span, 1) == kinds, 1.0, 0.0).astype(bf16)
            for k in range(KERNEL)
        ],
        axis=0,
    )
    first_t = jnp.dot(tt_ref[...], hot, preferred_element_type=f32)
    pos = pos - HALO - HALF
    first_t = jnp.where((pos >= 0) & (pos < WINDOW), elu(first_t), 0.0)
    f_ref[...] = first_t.T.astype(bf16).astype(f32)

    wide = COLS + 2 * HALO
    acc = jnp.zeros((PLANES + wide, W), f32)
    for k in range(KERNEL):
        lhs = jnp.concatenate([f_ref[pl.ds(k, PLANES), :], f_ref[pl.ds(128 + k, wide), :]], axis=0)
        acc = acc + jnp.dot(lhs.astype(bf16), w2_ref[pl.ds(k * W, W), :], preferred_element_type=f32)
    centre = jnp.concatenate([f_ref[pl.ds(HALF, PLANES), :], f_ref[pl.ds(128 + HALF, wide), :]], axis=0)
    second = (centre + elu(acc)).astype(bf16)

    nt = (((1,), (1,)), ((), ()))
    left = lax.dot_general(pr_ref[...], second[:PLANES], nt, preferred_element_type=f32)
    left = left.astype(bf16).astype(f32)
    cols_t = second[PLANES:]
    order_a = jnp.concatenate([cols_t[HALO:COLS], cols_t[:HALO]], axis=0)
    order_b = jnp.concatenate([cols_t[COLS + HALO :], cols_t[2 * HALO : COLS + HALO]], axis=0)
    right = jnp.concatenate(
        [lax.dot_general(pc_ref[...], o, nt, preferred_element_type=f32) for o in (order_a, order_b)],
        axis=1,
    )
    right = right.astype(bf16).astype(f32)

    lane2 = lax.broadcasted_iota(jnp.int32, (CH, 2 * COLS), 1)
    tile_col = jnp.where(
        lane2 < COLS,
        jnp.where(lane2 < COLS - HALO, lane2, lane2 - COLS),
        jnp.where(lane2 < COLS + HALO, lane2, lane2 - COLS),
    )
    col = col0 + tile_col
    col_ok = jnp.where((col >= 0) & (col < WINDOW), 1.0, 0.0).astype(bf16)

    def activate(x, plane):
        ok = col_ok
        if plane < HALO or plane >= PLANES - HALO:
            at = row0 - HALO + plane
            ok = col_ok * jnp.where((at >= 0) & (at < WINDOW), 1.0, 0.0).astype(bf16)
        return elu(x) * ok

    def rows_of(plane):
        return pl.ds(plane * CH, CH)

    for plane in range(1, PLANES - 1):
        x = (left[:, plane : plane + 1] + right).astype(bf16)
        x_ref[rows_of(plane), :] = x
        a_ref[rows_of(plane), :] = activate(x, plane)

    def layer(number, low, high, src, dst):
        d = 2**number
        weights = pw_ref[number]
        lanes = lax.broadcasted_iota(jnp.int32, (CH, COLS), 1)
        for plane in range(low, high):
            stack = [src[rows_of(plane + (t - 1) * d), :] for t in range(3)] + [x_ref[rows_of(plane), :]]
            y = jnp.dot(weights, jnp.concatenate(stack, axis=0), preferred_element_type=f32)
            before, here, after = y[:CH], y[CH : 2 * CH], y[2 * CH :]
            if dst is None:
                half = COLS // 2
                before = jnp.where((lanes < half - d) | (lanes >= COLS - d), before[:, :COLS], before[:, COLS:])
                here = jnp.where(lanes < half, here[:, :COLS], here[:, COLS:])
                after = jnp.where((lanes >= d) & (lanes < half + d), after[:, :COLS], after[:, COLS:])
                total = pltpu.roll(before, d, 1) + here + pltpu.roll(after, COLS - d, 1)
                s_ref[pl.ds(plane - HALO, CH, stride=ROWS), :] = total
            else:
                x = jnp.concatenate(
                    [
                        pltpu.roll(before[:, s], d, 1) + here[:, s] + pltpu.roll(after[:, s], COLS - d, 1)
                        for s in (slice(0, COLS), slice(COLS, 2 * COLS))
                    ],
                    axis=1,
                ).astype(bf16)
                x_ref[rows_of(plane), :] = x
                dst[rows_of(plane), :] = activate(x, plane)

    layer(0, 2, 62, a_ref, b_ref)
    layer(1, 4, 60, b_ref, a_ref)
    layer(2, 8, 56, a_ref, b_ref)
    layer(3, 16, 48, b_ref, None)
    out_ref[...] = s_ref[...].reshape(CH, ROWS, COLS).astype(bf16)


def local(residues, embed_table, conv_first, conv_second, proj_row, proj_col, pair_weights):
    vmem = pl.BlockSpec(memory_space=pltpu.VMEM)
    copies = jnp.broadcast_to(residues, (lax.axis_size("row"), 1, ROWS))
    every = lax.all_to_all(copies, "row", 0, 0, tiled=True)
    table = jnp.pad(embed_table, ((0, VOCAB_PAD - embed_table.shape[0]), (0, 0)))
    tt = pl.pallas_call(
        tables_kernel,
        in_specs=[vmem, pl.BlockSpec(memory_space=pl.ANY)],
        out_specs=vmem,
        out_shape=jax.ShapeDtypeStruct((W, KERNEL * VOCAB_PAD), bf16),
        scratch_shapes=[pltpu.VMEM((KERNEL * W, W), bf16), pltpu.SemaphoreType.DMA((len(PIECES) - 1,))],
        compiler_params=pltpu.CompilerParams(vmem_limit_bytes=60 * 2**20),
        cost_estimate=pl.CostEstimate(flops=2 * 32 * 4352 * 256, bytes_accessed=3 * 2**20, transcendentals=0),
    )(table, conv_first)
    pw = pair_weights.reshape(LAYERS, CH, 3, 3, CH).transpose(0, 3, 1, 2, 4).reshape(LAYERS, 3 * CH, 3 * CH)
    same = jnp.eye(3 * CH, CH, k=-CH, dtype=bf16)
    pw = jnp.concatenate([pw, jnp.broadcast_to(same, (LAYERS, *same.shape))], axis=2)
    return pl.pallas_call(
        pair_kernel,
        out_shape=jax.ShapeDtypeStruct((CH, ROWS, COLS), bf16),
        scratch_shapes=[
            pltpu.VMEM((384, W), f32),
            pltpu.VMEM((PLANES * CH, 2 * COLS), bf16),
            pltpu.VMEM((PLANES * CH, 2 * COLS), bf16),
            pltpu.VMEM((PLANES * CH, 2 * COLS), bf16),
            pltpu.VMEM((CH * ROWS, COLS), f32),
        ],
        compiler_params=pltpu.CompilerParams(vmem_limit_bytes=24 * 2**20),
        cost_estimate=pl.CostEstimate(flops=2 * 64 * 4096 * 2304, bytes_accessed=4 * 2**20, transcendentals=0),
    )(every, tt, conv_second, proj_row.T, proj_col.T, pw)


def solution(mesh):
    return jax.shard_map(
        local,
        mesh=mesh,
        in_specs=(P("row"), P(), P(), P(), P(), P(), P()),
        out_specs=P(None, "row", "col"),
        check_vma=False,
    )
```

```python
import jax
import jax.numpy as jnp
from jax import lax
from jax.experimental import pallas as pl
from jax.experimental.pallas import tpu as pltpu
from jax.sharding import PartitionSpec as P

KERNEL = 17
HALF = KERNEL // 2
LAYERS = 4
WINDOW = 1024
VOCAB_PAD = 32
PIECES = (0, 5, 9, 13, 17)
ROWS = 32
COLS = 128
HALO = 16
PLANES = ROWS + 2 * HALO
CH = 64
BLOCK = 16
W = 256
f32, bf16 = jnp.float32, jnp.bfloat16


def elu(v):
    return jnp.maximum(v, jnp.exp(jnp.minimum(v, 0.0)) - 1.0)


def tables_kernel(table_ref, w_hbm, out_ref, w_ref, sems):
    copies = [
        pltpu.make_async_copy(w_hbm.at[pl.ds(a * W, (b - a) * W)], w_ref.at[pl.ds(a * W, (b - a) * W)], sems.at[n])
        for n, (a, b) in enumerate(zip(PIECES, PIECES[1:]))
    ]
    for copy in copies:
        copy.start()
    parts = []
    for k in range(KERNEL):
        if k in PIECES:
            copies[PIECES.index(k)].wait()
        parts.append(jnp.dot(table_ref[...], w_ref[pl.ds(k * W, W), :], preferred_element_type=f32))
    out_ref[...] = jnp.concatenate(parts, axis=0).T.astype(bf16)


def pair_kernel(res_ref, tt_ref, w2_ref, pr_ref, pc_ref, pw_ref, out_ref, f_ref, x_ref, a_ref, b_ref, s_ref):
    row, column = lax.axis_index("row"), lax.axis_index("col")
    row0, col0 = row * ROWS, column * COLS
    blocks = res_ref.shape[0]
    span = 384

    def block(number):
        return res_ref[jnp.clip(number, 0, blocks - 1)]

    rows_blocks = [block(row - 1 + t) for t in range(3)]
    cols_blocks = [block(column * (COLS // ROWS) - 1 + t) for t in range(6)]
    res = jnp.concatenate(rows_blocks + rows_blocks[:1] + cols_blocks + cols_blocks[:2], axis=1)
    lane = lax.broadcasted_iota(jnp.int32, (1, span), 1)
    pos = jnp.where(lane < 128, row0 + lane, col0 + lane - 128)
    res = jnp.where((pos >= ROWS) & (pos < WINDOW + ROWS), res, -1)

    kinds = lax.broadcasted_iota(jnp.int32, (VOCAB_PAD, span), 0)
    hot = jnp.concatenate(
        [
            jnp.where(pltpu.roll(res, (span - k) % span, 1) == kinds, 1.0, 0.0).astype(bf16)
            for k in range(KERNEL)
        ],
        axis=0,
    )
    first_t = jnp.dot(tt_ref[...], hot, preferred_element_type=f32)
    pos = pos - HALO - HALF
    first_t = jnp.where((pos >= 0) & (pos < WINDOW), elu(first_t), 0.0)
    f_ref[...] = first_t.T.astype(bf16).astype(f32)

    wide = COLS + 2 * HALO
    acc = jnp.zeros((PLANES + wide, W), f32)
    for k in range(KERNEL):
        lhs = jnp.concatenate([f_ref[pl.ds(k, PLANES), :], f_ref[pl.ds(128 + k, wide), :]], axis=0)
        acc = acc + jnp.dot(lhs.astype(bf16), w2_ref[pl.ds(k * W, W), :], preferred_element_type=f32)
    centre = jnp.concatenate([f_ref[pl.ds(HALF, PLANES), :], f_ref[pl.ds(128 + HALF, wide), :]], axis=0)
    second = (centre + elu(acc)).astype(bf16)

    nt = (((1,), (1,)), ((), ()))
    left = lax.dot_general(pr_ref[...], second[:PLANES], nt, preferred_element_type=f32)
    left = left.astype(bf16).astype(f32)
    cols_t = second[PLANES:]
    order_a = jnp.concatenate([cols_t[HALO:COLS], cols_t[:HALO]], axis=0)
    order_b = jnp.concatenate([cols_t[COLS + HALO :], cols_t[2 * HALO : COLS + HALO]], axis=0)
    right = jnp.concatenate(
        [lax.dot_general(pc_ref[...], o, nt, preferred_element_type=f32) for o in (order_a, order_b)],
        axis=1,
    )
    right = right.astype(bf16).astype(f32)

    lane2 = lax.broadcasted_iota(jnp.int32, (BLOCK, 2 * COLS), 1)
    tile_col = jnp.where(
        lane2 < COLS,
        jnp.where(lane2 < COLS - HALO, lane2, lane2 - COLS),
        jnp.where(lane2 < COLS + HALO, lane2, lane2 - COLS),
    )
    col = col0 + tile_col
    col_ok = jnp.where((col >= 0) & (col < WINDOW), 1.0, 0.0).astype(bf16)

    def activate(x, plane):
        ok = col_ok
        if plane < HALO or plane >= PLANES - HALO:
            at = row0 - HALO + plane
            ok = col_ok * jnp.where((at >= 0) & (at < WINDOW), 1.0, 0.0).astype(bf16)
        return elu(x) * ok

    def rows_of(plane):
        return pl.ds(plane * CH, CH)

    for plane in range(1, PLANES - 1):
        for first in range(0, CH, BLOCK):
            block_of = slice(first, first + BLOCK)
            x = (left[block_of, plane : plane + 1] + right[block_of]).astype(bf16)
            x_ref[pl.ds(plane * CH + first, BLOCK), :] = x
            a_ref[pl.ds(plane * CH + first, BLOCK), :] = activate(x, plane)

    def layer(number, low, high, src, dst):
        d = 2**number
        weights = pw_ref[number]
        lanes = lax.broadcasted_iota(jnp.int32, (BLOCK, COLS), 1)
        for plane in range(low, high):
            stack = [src[rows_of(plane + (t - 1) * d), :] for t in range(3)] + [x_ref[rows_of(plane), :]]
            y = jnp.dot(weights, jnp.concatenate(stack, axis=0), preferred_element_type=f32)
            for first in range(0, CH, BLOCK):
                before, here, after = (y[3 * first + t * BLOCK : 3 * first + (t + 1) * BLOCK] for t in range(3))
                if dst is None:
                    half = COLS // 2
                    before = jnp.where((lanes < half - d) | (lanes >= COLS - d), before[:, :COLS], before[:, COLS:])
                    here = jnp.where(lanes < half, here[:, :COLS], here[:, COLS:])
                    after = jnp.where((lanes >= d) & (lanes < half + d), after[:, :COLS], after[:, COLS:])
                    total = pltpu.roll(before, d, 1) + here + pltpu.roll(after, COLS - d, 1)
                    s_ref[pl.ds(first * ROWS + plane - HALO, BLOCK, stride=ROWS), :] = total
                else:
                    x = jnp.concatenate(
                        [
                            pltpu.roll(before[:, s], d, 1) + here[:, s] + pltpu.roll(after[:, s], COLS - d, 1)
                            for s in (slice(0, COLS), slice(COLS, 2 * COLS))
                        ],
                        axis=1,
                    ).astype(bf16)
                    x_ref[pl.ds(plane * CH + first, BLOCK), :] = x
                    dst[pl.ds(plane * CH + first, BLOCK), :] = activate(x, plane)

    layer(0, 2, 62, a_ref, b_ref)
    layer(1, 4, 60, b_ref, a_ref)
    layer(2, 8, 56, a_ref, b_ref)
    layer(3, 16, 48, b_ref, None)
    out_ref[...] = s_ref[...].reshape(CH, ROWS, COLS).astype(bf16)


def local(residues, embed_table, conv_first, conv_second, proj_row, proj_col, pair_weights):
    vmem = pl.BlockSpec(memory_space=pltpu.VMEM)
    copies = jnp.broadcast_to(residues, (lax.axis_size("row"), 1, ROWS))
    every = lax.all_to_all(copies, "row", 0, 0, tiled=True)
    table = jnp.pad(embed_table, ((0, VOCAB_PAD - embed_table.shape[0]), (0, 0)))
    tt = pl.pallas_call(
        tables_kernel,
        in_specs=[vmem, pl.BlockSpec(memory_space=pl.ANY)],
        out_specs=vmem,
        out_shape=jax.ShapeDtypeStruct((W, KERNEL * VOCAB_PAD), bf16),
        scratch_shapes=[pltpu.VMEM((KERNEL * W, W), bf16), pltpu.SemaphoreType.DMA((len(PIECES) - 1,))],
        compiler_params=pltpu.CompilerParams(vmem_limit_bytes=40 * 2**20),
        cost_estimate=pl.CostEstimate(flops=2 * 32 * 4352 * 256, bytes_accessed=3 * 2**20, transcendentals=0),
    )(table, conv_first)
    tt, pair_weights = lax.optimization_barrier((tt, pair_weights))
    blocks = CH // BLOCK
    pw = pair_weights.reshape(LAYERS, blocks, BLOCK, 3, 3, CH).transpose(0, 1, 4, 2, 3, 5)
    pw = pw.reshape(LAYERS, 3 * CH, 3 * CH)
    same = jnp.eye(3 * CH, CH, k=-CH, dtype=bf16).reshape(3, blocks, BLOCK, CH)
    same = same.transpose(1, 0, 2, 3).reshape(3 * CH, CH)
    pw = jnp.concatenate([pw, jnp.broadcast_to(same, (LAYERS, *same.shape))], axis=2)
    return pl.pallas_call(
        pair_kernel,
        out_shape=jax.ShapeDtypeStruct((CH, ROWS, COLS), bf16),
        scratch_shapes=[
            pltpu.VMEM((384, W), f32),
            pltpu.VMEM((PLANES * CH, 2 * COLS), bf16),
            pltpu.VMEM((PLANES * CH, 2 * COLS), bf16),
            pltpu.VMEM((PLANES * CH, 2 * COLS), bf16),
            pltpu.VMEM((CH * ROWS, COLS), f32),
        ],
        compiler_params=pltpu.CompilerParams(vmem_limit_bytes=24 * 2**20),
        cost_estimate=pl.CostEstimate(flops=2 * 64 * 4096 * 2304, bytes_accessed=4 * 2**20, transcendentals=0),
    )(every, tt, conv_second, proj_row.T, proj_col.T, pw)


def solution(mesh):
    return jax.shard_map(
        local,
        mesh=mesh,
        in_specs=(P("row"), P(), P(), P(), P(), P(), P()),
        out_specs=P(None, "row", "col"),
        check_vma=False,
    )
```

```python
import jax
import jax.numpy as jnp
from jax import lax
from jax.experimental import pallas as pl
from jax.experimental.pallas import tpu as pltpu
from jax.sharding import PartitionSpec as P

KERNEL = 17
HALF = KERNEL // 2
LAYERS = 4
WINDOW = 1024
VOCAB_PAD = 32
PIECES = (0, 5, 9, 13, 17)
ROWS = 32
COLS = 128
HALO = 16
PLANES = ROWS + 2 * HALO
CH = 64
BLOCK = 16
W = 256
f32, bf16 = jnp.float32, jnp.bfloat16


def elu(v):
    return jnp.maximum(v, jnp.exp(jnp.minimum(v, 0.0)) - 1.0)


def tables_kernel(table_ref, w_hbm, out_ref, w_ref, sems):
    copies = [
        pltpu.make_async_copy(w_hbm.at[pl.ds(a * W, (b - a) * W)], w_ref.at[pl.ds(a * W, (b - a) * W)], sems.at[n])
        for n, (a, b) in enumerate(zip(PIECES, PIECES[1:]))
    ]
    for copy in copies:
        copy.start()
    parts = []
    for k in range(KERNEL):
        if k in PIECES:
            copies[PIECES.index(k)].wait()
        parts.append(jnp.dot(table_ref[...], w_ref[pl.ds(k * W, W), :], preferred_element_type=f32))
    out_ref[...] = jnp.concatenate(parts, axis=0).T.astype(bf16)


def pair_kernel(res_ref, tt_ref, w2_ref, pr_ref, pc_ref, pw_ref, out_ref, f_ref, x_ref, a_ref, b_ref, s_ref):
    row, column = lax.axis_index("row"), lax.axis_index("col")
    row0, col0 = row * ROWS, column * COLS
    blocks = res_ref.shape[0]
    span = 384

    def block(number):
        return res_ref[jnp.clip(number, 0, blocks - 1)]

    rows_blocks = [block(row - 1 + t) for t in range(3)]
    cols_blocks = [block(column * (COLS // ROWS) - 1 + t) for t in range(6)]
    res = jnp.concatenate(rows_blocks + rows_blocks[:1] + cols_blocks + cols_blocks[:2], axis=1)
    lane = lax.broadcasted_iota(jnp.int32, (1, span), 1)
    pos = jnp.where(lane < 128, row0 + lane, col0 + lane - 128)
    res = jnp.where((pos >= ROWS) & (pos < WINDOW + ROWS), res, -1)

    kinds = lax.broadcasted_iota(jnp.int32, (VOCAB_PAD, span), 0)
    hot = jnp.concatenate(
        [
            jnp.where(pltpu.roll(res, (span - k) % span, 1) == kinds, 1.0, 0.0).astype(bf16)
            for k in range(KERNEL)
        ],
        axis=0,
    )
    first_t = jnp.dot(tt_ref[...], hot, preferred_element_type=f32)
    pos = pos - HALO - HALF
    first_t = jnp.where((pos >= 0) & (pos < WINDOW), elu(first_t), 0.0)
    f_ref[...] = first_t.T.astype(bf16).astype(f32)

    wide = COLS + 2 * HALO
    acc = jnp.zeros((PLANES + wide, W), f32)
    for k in range(KERNEL):
        lhs = jnp.concatenate([f_ref[pl.ds(k, PLANES), :], f_ref[pl.ds(128 + k, wide), :]], axis=0)
        acc = acc + jnp.dot(lhs.astype(bf16), w2_ref[pl.ds(k * W, W), :], preferred_element_type=f32)
    centre = jnp.concatenate([f_ref[pl.ds(HALF, PLANES), :], f_ref[pl.ds(128 + HALF, wide), :]], axis=0)
    second = (centre + elu(acc)).astype(bf16)

    nt = (((1,), (1,)), ((), ()))
    left = lax.dot_general(pr_ref[...], second[:PLANES], nt, preferred_element_type=f32)
    left = left.astype(bf16).astype(f32)
    cols_t = second[PLANES:]
    order_a = jnp.concatenate([cols_t[HALO:COLS], cols_t[:HALO]], axis=0)
    order_b = jnp.concatenate([cols_t[COLS + HALO :], cols_t[2 * HALO : COLS + HALO]], axis=0)
    right = jnp.concatenate(
        [lax.dot_general(pc_ref[...], o, nt, preferred_element_type=f32) for o in (order_a, order_b)],
        axis=1,
    )
    right = right.astype(bf16).astype(f32)

    lane2 = lax.broadcasted_iota(jnp.int32, (BLOCK, 2 * COLS), 1)
    tile_col = jnp.where(
        lane2 < COLS,
        jnp.where(lane2 < COLS - HALO, lane2, lane2 - COLS),
        jnp.where(lane2 < COLS + HALO, lane2, lane2 - COLS),
    )
    col = col0 + tile_col
    col_ok = jnp.where((col >= 0) & (col < WINDOW), 1.0, 0.0).astype(bf16)

    def activate(x, plane):
        ok = col_ok
        if plane < HALO or plane >= PLANES - HALO:
            at = row0 - HALO + plane
            ok = col_ok * jnp.where((at >= 0) & (at < WINDOW), 1.0, 0.0).astype(bf16)
        return elu(x) * ok

    def rows_of(plane):
        return pl.ds(plane * CH, CH)

    def outer_sum(plane):
        for first in range(0, CH, BLOCK):
            block_of = slice(first, first + BLOCK)
            x = (left[block_of, plane : plane + 1] + right[block_of]).astype(bf16)
            x_ref[pl.ds(plane * CH + first, BLOCK), :] = x
            a_ref[pl.ds(plane * CH + first, BLOCK), :] = activate(x, plane)

    for plane in range(1, 5):
        outer_sum(plane)

    def layer(number, low, high, src, dst):
        d = 2**number
        weights = pw_ref[number]
        lanes = lax.broadcasted_iota(jnp.int32, (BLOCK, COLS), 1)
        def product(plane):
            stack = [src[rows_of(plane + (t - 1) * d), :] for t in range(3)] + [x_ref[rows_of(plane), :]]
            return jnp.dot(weights, jnp.concatenate(stack, axis=0), preferred_element_type=f32)

        ready = product(low)
        for plane in range(low, high):
            if number == 0 and plane + 3 < PLANES - 1:
                outer_sum(plane + 3)
            y, ready = ready, product(plane + 1) if plane + 1 < high else None
            for first in range(0, CH, BLOCK):
                before, here, after = (y[3 * first + t * BLOCK : 3 * first + (t + 1) * BLOCK] for t in range(3))
                if dst is None:
                    half = COLS // 2
                    before = jnp.where((lanes < half - d) | (lanes >= COLS - d), before[:, :COLS], before[:, COLS:])
                    here = jnp.where(lanes < half, here[:, :COLS], here[:, COLS:])
                    after = jnp.where((lanes >= d) & (lanes < half + d), after[:, :COLS], after[:, COLS:])
                    total = pltpu.roll(before, d, 1) + here + pltpu.roll(after, COLS - d, 1)
                    s_ref[pl.ds(first * ROWS + plane - HALO, BLOCK, stride=ROWS), :] = total
                else:
                    x = jnp.concatenate(
                        [
                            pltpu.roll(before[:, s], d, 1) + here[:, s] + pltpu.roll(after[:, s], COLS - d, 1)
                            for s in (slice(0, COLS), slice(COLS, 2 * COLS))
                        ],
                        axis=1,
                    ).astype(bf16)
                    x_ref[pl.ds(plane * CH + first, BLOCK), :] = x
                    dst[pl.ds(plane * CH + first, BLOCK), :] = activate(x, plane)

    layer(0, 2, 62, a_ref, b_ref)
    layer(1, 4, 60, b_ref, a_ref)
    layer(2, 8, 56, a_ref, b_ref)
    layer(3, 16, 48, b_ref, None)
    out_ref[...] = s_ref[...].reshape(CH, ROWS, COLS).astype(bf16)


def local(residues, embed_table, conv_first, conv_second, proj_row, proj_col, pair_weights):
    vmem = pl.BlockSpec(memory_space=pltpu.VMEM)
    copies = jnp.broadcast_to(residues, (lax.axis_size("row"), 1, ROWS))
    every = lax.all_to_all(copies, "row", 0, 0, tiled=True)
    table = jnp.pad(embed_table, ((0, VOCAB_PAD - embed_table.shape[0]), (0, 0)))
    tt = pl.pallas_call(
        tables_kernel,
        in_specs=[vmem, pl.BlockSpec(memory_space=pl.ANY)],
        out_specs=vmem,
        out_shape=jax.ShapeDtypeStruct((W, KERNEL * VOCAB_PAD), bf16),
        scratch_shapes=[pltpu.VMEM((KERNEL * W, W), bf16), pltpu.SemaphoreType.DMA((len(PIECES) - 1,))],
        compiler_params=pltpu.CompilerParams(vmem_limit_bytes=40 * 2**20),
        cost_estimate=pl.CostEstimate(flops=2 * 32 * 4352 * 256, bytes_accessed=3 * 2**20, transcendentals=0),
    )(table, conv_first)
    tt, pair_weights = lax.optimization_barrier((tt, pair_weights))
    blocks = CH // BLOCK
    pw = pair_weights.reshape(LAYERS, blocks, BLOCK, 3, 3, CH).transpose(0, 1, 4, 2, 3, 5)
    pw = pw.reshape(LAYERS, 3 * CH, 3 * CH)
    same = jnp.eye(3 * CH, CH, k=-CH, dtype=bf16).reshape(3, blocks, BLOCK, CH)
    same = same.transpose(1, 0, 2, 3).reshape(3 * CH, CH)
    pw = jnp.concatenate([pw, jnp.broadcast_to(same, (LAYERS, *same.shape))], axis=2)
    return pl.pallas_call(
        pair_kernel,
        out_shape=jax.ShapeDtypeStruct((CH, ROWS, COLS), bf16),
        scratch_shapes=[
            pltpu.VMEM((384, W), f32),
            pltpu.VMEM((PLANES * CH, 2 * COLS), bf16),
            pltpu.VMEM((PLANES * CH, 2 * COLS), bf16),
            pltpu.VMEM((PLANES * CH, 2 * COLS), bf16),
            pltpu.VMEM((CH * ROWS, COLS), f32),
        ],
        compiler_params=pltpu.CompilerParams(vmem_limit_bytes=24 * 2**20),
        cost_estimate=pl.CostEstimate(flops=2 * 64 * 4096 * 2304, bytes_accessed=4 * 2**20, transcendentals=0),
    )(every, tt, conv_second, proj_row.T, proj_col.T, pw)


def solution(mesh):
    return jax.shard_map(
        local,
        mesh=mesh,
        in_specs=(P("row"), P(), P(), P(), P(), P(), P()),
        out_specs=P(None, "row", "col"),
        check_vma=False,
    )
```
